512 devices in a mesh: dp: 32 (over z_lo, y, core), fsdp: 16 (over z_hi, x).
Axes of the slice: x: 4, y: 4, z: 16 (z_hi: 4, z_lo: 4; z = z_hi * 4 + z_lo), core: 2. Of those that a mesh axis runs over, the one named last changes fastest.
Arguments:
- activations: bfloat16 [8192, 4096], P('dp', 'fsdp'), may hold values from -6 to 6
- output_grads: bfloat16 [8192, 4096], P('dp', 'fsdp'), may hold values from -6 to 6
- basis: bfloat16 [4096, 1024], P('fsdp'), may hold values from -0.09375 to 0.09375
- weight: bfloat16 [4096, 4096], P('fsdp'), may hold values from -0.09375 to 0.09375
- first_moment: float32 [4096, 1024], P(('fsdp', 'dp')), may hold values from -0.06 to 0.06
- second_moment: float32 [4096, 1024], P(('fsdp', 'dp')), may hold values from 1e-07 to 1e-05
Outputs:
- new_weight: bfloat16 [4096, 4096], P('fsdp')
- new_first: float32 [4096, 1024], P(('fsdp', 'dp'))
- new_second: float32 [4096, 1024], P(('fsdp', 'dp'))
The draws below stay inside these ranges and needn't reach their ends.
All inputs are finite; a program needn't handle non-finite values.
Results may differ from the reference program's by a relative error of at most 0.0036.
Values may be sent and summed in bfloat16 or wider, within the bound.
No kernel may reach another device: no remote copies, remote signals or barrier semaphores. Data moves between devices by JAX's collectives and lax.ppermute only.
A program may use at most 64 MiB of HBM per device.

```python
import math
import jax
import jax.numpy as jnp
from jax import lax

D = 4096
RANK = 1024
TOKENS = 8192


def with_spikes(result, key, source, target, shards_of, factor):
    def block_of(dim):
        return (jnp.arange(result.shape[dim]) // (result.shape[dim] // shards_of)).reshape((-1,) + (1,) * (result.ndim - 1 - dim))

    first = jax.random.permutation(key, shards_of)[block_of(target)]
    other_side = (block_of(target) + shards_of // 2) % shards_of
    return jnp.where((block_of(source) == first) | (block_of(source) == other_side), factor * result, result)


def shard_levels(stream_key, extent, shards, low, high):
    def one(position, blocks):
        draws = jax.random.uniform(jax.random.fold_in(jax.random.fold_in(stream_key, 6), position), (blocks,), jnp.float32, low / len(shards), high / len(shards))
        return jnp.repeat(jnp.exp(draws), extent[position] // blocks).reshape((-1,) + (1,) * (len(extent) - position - 1))

    gain = one(*shards[0])
    for cut in shards[1:]:
        gain = gain * one(*cut)
    return gain


def noise(rng, shape, spread, reach, split=(), dtype=jnp.bfloat16):
    array = jax.random.normal(rng, shape, jnp.float32) * spread
    if len(split) > 0:
        array = shard_levels(rng, shape, split, -0.22, 0.18) * array
    return jnp.clip(array, min=-reach, max=reach).astype(dtype)


def bell_draw_with(stream_key, extent, spread, bound, split, heavy, kind=jnp.bfloat16):
    drawn = spread * jax.random.normal(stream_key, extent, jnp.float32)
    if split:
        drawn = drawn * shard_levels(stream_key, extent, split, -0.22, 0.18)
    return jnp.clip(with_spikes(drawn, jax.random.fold_in(stream_key, 3), *heavy), -bound, bound).astype(kind)


def setup_inputs(seed: int = 0) -> dict:
    seeds = jax.random.split(jax.random.key(seed), 7)
    activations = noise(seeds[0], (TOKENS, D), 1.0, 6.0, ((0, 32), (1, 16)))
    output_grads = bell_draw_with(seeds[1], (TOKENS, D), 1.0, 6.0, ((0, 32), (1, 16)), (0, 1, 32, 2.75))
    basis = noise(seeds[2], (D, RANK), D ** -0.5, 0.09375, ((0, 16),))
    weight = noise(seeds[3], (D, D), D ** -0.5, 0.09375, ((0, 16),))
    first_moment = noise(seeds[4], (D, RANK), 0.01, 0.06, ((0, 512),), jnp.float32)
    second_moment = jnp.clip(jnp.exp(math.log(9.999999747378752e-06) - 4.6051701 * jax.random.uniform(seeds[5], (D, RANK), jnp.float32) ** shard_levels(seeds[5], (D, RANK), ((0, 512),), -0.2, 0.2)), 1.0000000116860974e-07, 9.999999747378752e-06)
    return dict(activations=activations, output_grads=output_grads, basis=basis, weight=weight, first_moment=first_moment, second_moment=second_moment)


first_decay = 0.9
second_decay = 0.999
first_fix = 1.0 - 0.9 ** 10
second_fix = 1.0 - 0.999 ** 10
step_rate = 0.01
tiny_eps = 1e-08

def reference(activations, output_grads, basis, weight, first_moment, second_moment):
    projected = jnp.dot(activations, basis, preferred_element_type=jnp.float32).astype(jnp.bfloat16)
    low_grad = lax.dot_general(output_grads, projected, (((0,), (0,)), ((), ())), preferred_element_type=jnp.float32) / TOKENS
    new_first = first_decay * first_moment + (1.0 - first_decay) * low_grad
    new_second = second_decay * second_moment + (1.0 - second_decay) * low_grad * low_grad
    update = (new_first / first_fix / (jnp.sqrt(new_second / second_fix) + tiny_eps)).astype(jnp.bfloat16)
    decoded = lax.dot_general(update, basis, (((1,), (1,)), ((), ())), preferred_element_type=jnp.float32)
    new_weight = (weight.astype(jnp.float32) - step_rate * decoded).astype(jnp.bfloat16)
    return (new_weight, new_first, new_second)
```

```python
import jax
import jax.numpy as jnp
from jax import lax
from jax.experimental import pallas as pl
from jax.experimental.pallas import tpu as pltpu
from jax.sharding import Mesh
from jax.sharding import PartitionSpec as P

first_decay = 0.9
second_decay = 0.999
first_fix = 1.0 - 0.9**10
second_fix = 1.0 - 0.999**10
step_rate = 0.01
tiny_eps = 1e-08

AXES = ("zl", "y", "c", "zh", "x")
SIZES = (4, 4, 2, 4, 4)
DP = ("zl", "y", "c")
FSDP = ("zh", "x")
TOKENS = 8192


def exchange_sum(value, axis):
    size = lax.axis_size(axis)
    rows, cols = value.shape
    parts = value.astype(jnp.bfloat16).reshape(size, rows // size, cols)
    parts = lax.all_to_all(parts, axis, 0, 0, tiled=True)
    return jnp.sum(parts.astype(jnp.float32), axis=0)


def gather(value, axis):
    size = lax.axis_size(axis)
    copies = jnp.broadcast_to(value[None], (size,) + value.shape)
    return lax.all_to_all(copies, axis, 0, 0, tiled=True).reshape(
        size * value.shape[0], value.shape[1]
    )


def decode_kernel(core_ref, update_ref, basis_ref, weight_ref, out_ref):
    decoded = lax.dot_general(
        update_ref[...],
        basis_ref[...],
        (((1,), (1,)), ((), ())),
        preferred_element_type=jnp.float32,
    )
    first = core_ref[0] == 0
    for g in range(2):
        left = weight_ref[:, 256 * g : 256 * g + 128]
        right = weight_ref[:, 256 * g + 128 : 256 * g + 256]
        old = jnp.where(first, left.astype(jnp.float32), right.astype(jnp.float32))
        out_ref[:, 128 * g : 128 * g + 128] = (
            old - step_rate * decoded[:, 128 * g : 128 * g + 128]
        ).astype(out_ref.dtype)


def decode_half(core, updates, basis_half, weight):
    rows, rank = updates.shape
    cols = basis_half.shape[0]
    return pl.pallas_call(
        decode_kernel,
        grid_spec=pltpu.PrefetchScalarGridSpec(
            num_scalar_prefetch=1,
            grid=(cols // 256,),
            in_specs=[
                pl.BlockSpec((rows, rank), lambda i, core: (0, 0)),
                pl.BlockSpec((256, rank), lambda i, core: (i, 0)),
                pl.BlockSpec((rows, 512), lambda i, core: (0, i)),
            ],
            out_specs=pl.BlockSpec((rows, 256), lambda i, core: (0, i)),
        ),
        out_shape=jax.ShapeDtypeStruct((rows, cols), weight.dtype),
        compiler_params=pltpu.CompilerParams(vmem_limit_bytes=24 * 1024 * 1024),
        name="decode_half",
    )(core, updates, basis_half, weight)


def merge_kernel(core_ref, mine_ref, other_ref, out_ref):
    first = core_ref[0] == 0
    for g in range(mine_ref.shape[1] // 128):
        mine = mine_ref[:, 128 * g : 128 * g + 128].astype(jnp.float32)
        other = other_ref[:, 128 * g : 128 * g + 128].astype(jnp.float32)
        out_ref[:, 256 * g : 256 * g + 128] = jnp.where(first, mine, other).astype(out_ref.dtype)
        out_ref[:, 256 * g + 128 : 256 * g + 256] = jnp.where(first, other, mine).astype(
            out_ref.dtype
        )


def merge(core, mine, other):
    rows, cols = mine.shape
    return pl.pallas_call(
        merge_kernel,
        grid_spec=pltpu.PrefetchScalarGridSpec(
            num_scalar_prefetch=1,
            grid=(cols // 512,),
            in_specs=[
                pl.BlockSpec((rows, 512), lambda i, core: (0, i)),
                pl.BlockSpec((rows, 512), lambda i, core: (0, i)),
            ],
            out_specs=pl.BlockSpec((rows, 1024), lambda i, core: (0, i)),
        ),
        out_shape=jax.ShapeDtypeStruct((rows, 2 * cols), mine.dtype),
        compiler_params=pltpu.CompilerParams(vmem_limit_bytes=24 * 1024 * 1024),
        name="merge_halves",
    )(core, mine, other)


def local(activations, output_grads, basis, weight, first_moment, second_moment):
    core = lax.axis_index("c")
    half = basis.shape[0] // 2
    my_half = lax.dynamic_slice_in_dim(basis, core * half, half, 0)
    basis_half = lax.all_gather(my_half, FSDP, axis=0, tiled=True)

    partial_product = jnp.dot(activations, basis, preferred_element_type=jnp.float32)
    shared = exchange_sum(exchange_sum(partial_product, "x"), "zh").astype(jnp.bfloat16)
    projected = gather(gather(shared, "zh"), "x")
    local_term = (
        lax.dot_general(
            output_grads, projected, (((0,), (0,)), ((), ())), preferred_element_type=jnp.float32
        )
        / TOKENS
    )
    low_grad = exchange_sum(local_term, DP)
    new_first = first_decay * first_moment + (1.0 - first_decay) * low_grad
    new_second = second_decay * second_moment + (1.0 - second_decay) * low_grad * low_grad
    update = (new_first / first_fix / (jnp.sqrt(new_second / second_fix) + tiny_eps)).astype(
        jnp.bfloat16
    )
    all_updates = gather(update, DP)
    which = jnp.full((1,), core, jnp.int32)
    mine = decode_half(which, all_updates, basis_half, weight)
    other = lax.ppermute(mine, "c", [(0, 1), (1, 0)])
    return (merge(which, mine, other), new_first, new_second)


def solution(mesh):
    named = Mesh(mesh.devices.reshape(SIZES), AXES)
    return jax.shard_map(
        local,
        mesh=named,
        in_specs=(
            P(DP, FSDP),
            P(DP, FSDP),
            P(FSDP, None),
            P(FSDP, None),
            P(FSDP + DP, None),
            P(FSDP + DP, None),
        ),
        out_specs=(P(FSDP, None), P(FSDP + DP, None), P(FSDP + DP, None)),
        check_vma=False,
    )
```

```python
import jax
import jax.numpy as jnp
from jax import lax
from jax.experimental import pallas as pl
from jax.experimental.pallas import tpu as pltpu
from jax.sharding import Mesh
from jax.sharding import PartitionSpec as P

first_decay = 0.9
second_decay = 0.999
first_fix = 1.0 - 0.9**10
second_fix = 1.0 - 0.999**10
step_rate = 0.01
tiny_eps = 1e-08

AXES = ("zl", "y", "c", "zh", "x")
SIZES = (4, 4, 2, 4, 4)
DP = ("zl", "y", "c")
FSDP = ("zh", "x")
TOKENS = 8192


def exchange_sum(value, axis):
    size = lax.axis_size(axis)
    rows, cols = value.shape
    parts = value.astype(jnp.bfloat16).reshape(size, rows // size, cols)
    parts = lax.all_to_all(parts, axis, 0, 0, tiled=True)
    return jnp.sum(parts.astype(jnp.float32), axis=0)


def gather(value, axis):
    size = lax.axis_size(axis)
    copies = jnp.broadcast_to(value[None], (size,) + value.shape)
    return lax.all_to_all(copies, axis, 0, 0, tiled=True).reshape(
        size * value.shape[0], value.shape[1]
    )


def decode_kernel(update_ref, basis_ref, weight_ref, out_ref):
    rank = update_ref.shape[-1]
    cols = out_ref.shape[1]
    updates = update_ref[...].reshape(-1, rank)
    decoded = lax.dot_general(
        updates,
        basis_ref[...].reshape(cols, rank),
        (((1,), (1,)), ((), ())),
        preferred_element_type=jnp.float32,
    )
    decoded = decoded.reshape(2, -1, 8, cols)
    decoded = jnp.stack([decoded[0], decoded[1]], axis=1).reshape(-1, cols)
    out_ref[...] = (weight_ref[...].astype(jnp.float32) - step_rate * decoded).astype(
        out_ref.dtype
    )


def decode(updates, basis_pieces, weight):
    rows, cols = weight.shape
    two, ys, xs, zhs, piece, rank = basis_pieces.shape
    width = two * ys * piece
    return pl.pallas_call(
        decode_kernel,
        grid=(cols // width,),
        in_specs=[
            pl.BlockSpec(updates.shape, lambda i: (0, 0, 0)),
            pl.BlockSpec((two, ys, 1, 1, piece, rank), lambda i: (0, 0, i % xs, i // xs, 0, 0)),
            pl.BlockSpec((rows, width), lambda i: (0, i)),
        ],
        out_specs=pl.BlockSpec((rows, width), lambda i: (0, i)),
        out_shape=jax.ShapeDtypeStruct((rows, cols), weight.dtype),
        compiler_params=pltpu.CompilerParams(vmem_limit_bytes=56 * 1024 * 1024),
        name="decode",
    )(updates, basis_pieces, weight)


def local(activations, output_grads, basis, weight, first_moment, second_moment):
    core = lax.axis_index("c")
    piece = basis.shape[0] // 8
    mine = lax.dynamic_slice_in_dim(basis, (core * 4 + lax.axis_index("y")) * piece, piece, 0)
    mine = lax.all_gather(mine, "zh", axis=0, tiled=True)
    basis_pieces = lax.all_gather(mine, ("c", "y", "x"), axis=0, tiled=True).reshape(
        2, 4, 4, 4, piece, -1
    )

    partial_product = jnp.dot(activations, basis, preferred_element_type=jnp.float32)
    over_x = exchange_sum(partial_product, "x").astype(jnp.bfloat16)
    rows, rank = over_x.shape
    over_all = gather(over_x, "zh").reshape(4, rows, rank)
    block = jnp.sum(over_all.astype(jnp.float32), axis=0).astype(jnp.bfloat16)
    projected = gather(block, "x")
    local_term = (
        lax.dot_general(
            output_grads, projected, (((0,), (0,)), ((), ())), preferred_element_type=jnp.float32
        )
        / TOKENS
    )
    parts = local_term.reshape(-1, 2, 8, rank)
    keep = lax.dynamic_index_in_dim(parts, core, 1, keepdims=False)
    send = lax.dynamic_index_in_dim(parts, 1 - core, 1, keepdims=False).astype(jnp.bfloat16)
    sent = lax.all_gather(send, "c", axis=0)
    received = lax.dynamic_index_in_dim(sent, 1 - core, 0, keepdims=False)
    chip_term = keep + received.astype(jnp.float32)
    low_grad = exchange_sum(chip_term.reshape(-1, rank), ("zl", "y"))
    new_first = first_decay * first_moment + (1.0 - first_decay) * low_grad
    new_second = second_decay * second_moment + (1.0 - second_decay) * low_grad * low_grad
    update = (new_first / first_fix / (jnp.sqrt(new_second / second_fix) + tiny_eps)).astype(
        jnp.bfloat16
    )
    updates = lax.all_gather(gather(update, ("zl", "y")), "c", axis=0)
    return (decode(updates, basis_pieces, weight), new_first, new_second)


def solution(mesh):
    named = Mesh(mesh.devices.reshape(SIZES), AXES)
    return jax.shard_map(
        local,
        mesh=named,
        in_specs=(
            P(DP, FSDP),
            P(DP, FSDP),
            P(FSDP, None),
            P(FSDP, None),
            P(FSDP + DP, None),
            P(FSDP + DP, None),
        ),
        out_specs=(P(FSDP, None), P(FSDP + DP, None), P(FSDP + DP, None)),
        check_vma=False,
    )
```

```python
import jax
import jax.numpy as jnp
from jax import lax
from jax.experimental import pallas as pl
from jax.experimental.pallas import tpu as pltpu
from jax.sharding import Mesh
from jax.sharding import PartitionSpec as P

first_decay = 0.9
second_decay = 0.999
first_fix = 1.0 - 0.9**10
second_fix = 1.0 - 0.999**10
step_rate = 0.01
tiny_eps = 1e-08

AXES = ("zl", "y", "c", "zh", "x")
SIZES = (4, 4, 2, 4, 4)
DP = ("zl", "y", "c")
FSDP = ("zh", "x")
TOKENS = 8192


def exchange_sum(value, axis):
    size = lax.axis_size(axis)
    rows, cols = value.shape
    parts = value.astype(jnp.bfloat16).reshape(size, rows // size, cols)
    parts = lax.all_to_all(parts, axis, 0, 0, tiled=True)
    return jnp.sum(parts.astype(jnp.float32), axis=0)


def gather(value, axis):
    size = lax.axis_size(axis)
    copies = jnp.broadcast_to(value[None], (size,) + value.shape)
    return lax.all_to_all(copies, axis, 0, 0, tiled=True).reshape(
        size * value.shape[0], value.shape[1]
    )


STEP = 2


def decode_kernel(update_ref, basis_ref, weight_ref, out_ref, new, sems):
    two, ys, xs, zhs, piece, rank = basis_ref.shape
    shard = two * ys * piece
    cols = STEP * shard

    def copy_out(i):
        where = pl.ds(i * cols, cols)
        return pltpu.make_async_copy(new.at[:, where], out_ref.at[:, where], sems.at[i])

    updates = update_ref[...].reshape(-1, rank)
    steps = xs * zhs // STEP
    for i in range(steps):
        shards = [
            basis_ref[:, :, f % xs, f // xs].reshape(shard, rank)
            for f in range(i * STEP, (i + 1) * STEP)
        ]
        decoded = lax.dot_general(
            updates,
            jnp.concatenate(shards, axis=0),
            (((1,), (1,)), ((), ())),
            preferred_element_type=jnp.float32,
        )
        decoded = decoded.reshape(2, -1, 8, cols)
        decoded = jnp.stack([decoded[0], decoded[1]], axis=1).reshape(-1, cols)
        old = weight_ref[:, i * cols : (i + 1) * cols].astype(jnp.float32)
        new[:, i * cols : (i + 1) * cols] = (old - step_rate * decoded).astype(new.dtype)
        copy_out(i).start()
    for i in range(steps):
        copy_out(i).wait()


def decode(updates, basis_pieces, weight):
    steps = basis_pieces.shape[2] * basis_pieces.shape[3] // STEP
    return pl.pallas_call(
        decode_kernel,
        in_specs=[pl.BlockSpec(memory_space=pltpu.VMEM)] * 3,
        out_specs=pl.BlockSpec(memory_space=pl.ANY),
        out_shape=jax.ShapeDtypeStruct(weight.shape, weight.dtype),
        scratch_shapes=[
            pltpu.VMEM(weight.shape, weight.dtype),
            pltpu.SemaphoreType.DMA((steps,)),
        ],
        compiler_params=pltpu.CompilerParams(vmem_limit_bytes=24 * 1024 * 1024),
        name="decode",
    )(updates, basis_pieces, weight)


def local(activations, output_grads, basis, weight, first_moment, second_moment):
    core = lax.axis_index("c")
    piece = basis.shape[0] // 8
    mine = lax.dynamic_slice_in_dim(basis, (core * 4 + lax.axis_index("y")) * piece, piece, 0)

    partial_product = jnp.dot(activations, basis, preferred_element_type=jnp.float32)
    over_x = exchange_sum(partial_product, "x").astype(jnp.bfloat16)
    rank = over_x.shape[1]
    parts = over_x.reshape(4, -1, rank)
    rows = parts.shape[1]
    copies = jnp.broadcast_to(mine[None], (4,) + mine.shape)
    both = lax.all_to_all(jnp.concatenate([parts, copies], axis=1), "zh", 0, 0, tiled=True)
    basis_pieces = lax.all_gather(
        both[:, rows:].reshape(-1, rank), ("c", "y", "x"), axis=0, tiled=True
    ).reshape(2, 4, 4, 4, piece, rank)
    block = jnp.sum(both[:, :rows].astype(jnp.float32), axis=0).astype(jnp.bfloat16)
    projected = gather(gather(block, "zh"), "x")
    local_term = (
        lax.dot_general(
            output_grads, projected, (((0,), (0,)), ((), ())), preferred_element_type=jnp.float32
        )
        / TOKENS
    )
    parts = local_term.reshape(-1, 2, 8, rank)
    keep = lax.dynamic_index_in_dim(parts, core, 1, keepdims=False)
    send = lax.dynamic_index_in_dim(parts, 1 - core, 1, keepdims=False).astype(jnp.bfloat16)
    sent = lax.all_gather(send, "c", axis=0)
    received = lax.dynamic_index_in_dim(sent, 1 - core, 0, keepdims=False)
    chip_term = keep + received.astype(jnp.float32)
    low_grad = exchange_sum(chip_term.reshape(-1, rank), ("zl", "y"))
    new_first = first_decay * first_moment + (1.0 - first_decay) * low_grad
    new_second = second_decay * second_moment + (1.0 - second_decay) * low_grad * low_grad
    update = (new_first / first_fix / (jnp.sqrt(new_second / second_fix) + tiny_eps)).astype(
        jnp.bfloat16
    )
    updates = lax.all_gather(gather(update, ("zl", "y")), "c", axis=0)
    return (decode(updates, basis_pieces, weight), new_first, new_second)


def solution(mesh):
    named = Mesh(mesh.devices.reshape(SIZES), AXES)
    return jax.shard_map(
        local,
        mesh=named,
        in_specs=(
            P(DP, FSDP),
            P(DP, FSDP),
            P(FSDP, None),
            P(FSDP, None),
            P(FSDP + DP, None),
            P(FSDP + DP, None),
        ),
        out_specs=(P(FSDP, None), P(FSDP + DP, None), P(FSDP + DP, None)),
        check_vma=False,
    )
```

```python
import jax
import jax.numpy as jnp
from jax import lax
from jax.experimental import pallas as pl
from jax.experimental.pallas import tpu as pltpu
from jax.sharding import Mesh
from jax.sharding import PartitionSpec as P

first_decay = 0.9
second_decay = 0.999
first_fix = 1.0 - 0.9**10
second_fix = 1.0 - 0.999**10
step_rate = 0.01
tiny_eps = 1e-08

AXES = ("zl", "y", "c", "zh", "x")
SIZES = (4, 4, 2, 4, 4)
DP = ("zl", "y", "c")
FSDP = ("zh", "x")
TOKENS = 8192


def exchange_sum(value, axis):
    size = lax.axis_size(axis)
    rows, cols = value.shape
    parts = value.astype(jnp.bfloat16).reshape(size, rows // size, cols)
    parts = lax.all_to_all(parts, axis, 0, 0, tiled=True)
    return jnp.sum(parts.astype(jnp.float32), axis=0)


def permute_sum(value, axis):
    size = lax.axis_size(axis)
    me = lax.axis_index(axis)
    rows = value.shape[0] // size
    total = lax.dynamic_slice_in_dim(value, me * rows, rows, 0)
    for step in range(1, size):
        block = lax.dynamic_slice_in_dim(value, lax.rem(me + step, size) * rows, rows, 0)
        got = lax.ppermute(
            block.astype(jnp.bfloat16), axis, [(i, (i + step) % size) for i in range(size)]
        )
        total += got.astype(jnp.float32)
    return total


def gather(value, axis):
    size = lax.axis_size(axis)
    copies = jnp.broadcast_to(value[None], (size,) + value.shape)
    return lax.all_to_all(copies, axis, 0, 0, tiled=True).reshape(
        size * value.shape[0], value.shape[1]
    )


STEP = 2


def decode_kernel(update_ref, left_ref, right_ref, weight_ref, out_ref, new, sems):
    two, ys, xs, zhs, piece, half = left_ref.shape
    rank = update_ref.shape[-1]
    shard = two * ys * piece
    cols = STEP * shard

    def copy_out(i):
        where = pl.ds(i * cols, cols)
        return pltpu.make_async_copy(new.at[:, where], out_ref.at[:, where], sems.at[i])

    updates = update_ref[...].reshape(-1, rank)
    steps = xs * zhs // STEP
    for i in range(steps):
        decoded = 0.0
        for k, basis_ref in enumerate((left_ref, right_ref)):
            shards = [
                basis_ref[:, :, f % xs, f // xs].reshape(shard, half)
                for f in range(i * STEP, (i + 1) * STEP)
            ]
            decoded += lax.dot_general(
                updates[:, k * half : (k + 1) * half],
                jnp.concatenate(shards, axis=0),
                (((1,), (1,)), ((), ())),
                preferred_element_type=jnp.float32,
            )
        decoded = decoded.reshape(2, -1, 8, cols)
        decoded = jnp.stack([decoded[0], decoded[1]], axis=1).reshape(-1, cols)
        old = weight_ref[:, i * cols : (i + 1) * cols].astype(jnp.float32)
        new[:, i * cols : (i + 1) * cols] = (old - step_rate * decoded).astype(new.dtype)
        copy_out(i).start()
    for i in range(steps):
        copy_out(i).wait()


def decode(updates, basis_pieces, weight):
    left, right = basis_pieces
    steps = left.shape[2] * left.shape[3] // STEP
    return pl.pallas_call(
        decode_kernel,
        in_specs=[pl.BlockSpec(memory_space=pltpu.VMEM)] * 4,
        out_specs=pl.BlockSpec(memory_space=pl.ANY),
        out_shape=jax.ShapeDtypeStruct(weight.shape, weight.dtype),
        scratch_shapes=[
            pltpu.VMEM(weight.shape, weight.dtype),
            pltpu.SemaphoreType.DMA((steps,)),
        ],
        compiler_params=pltpu.CompilerParams(vmem_limit_bytes=24 * 1024 * 1024),
        name="decode",
    )(updates, left, right, weight)


def local(activations, output_grads, basis, weight, first_moment, second_moment):
    core = lax.axis_index("c")
    piece = basis.shape[0] // 8
    mine = lax.dynamic_slice_in_dim(basis, (core * 4 + lax.axis_index("y")) * piece, piece, 0)
    mine = gather(mine, "zh")

    partial_product = jnp.dot(activations, basis, preferred_element_type=jnp.float32)
    over_x = permute_sum(partial_product, "x").astype(jnp.bfloat16)
    over_x, mine = lax.optimization_barrier((over_x, mine))
    half = mine.shape[1] // 2
    basis_pieces = [
        lax.all_gather(mine[:, k * half : (k + 1) * half], ("c", "y", "x"), axis=0, tiled=True)
        .reshape(2, 4, 4, 4, piece, half)
        for k in range(2)
    ]

    block = exchange_sum(over_x, "zh").astype(jnp.bfloat16)
    projected = gather(gather(block, "zh"), "x")
    rank = projected.shape[1]
    local_term = (
        lax.dot_general(
            output_grads, projected, (((0,), (0,)), ((), ())), preferred_element_type=jnp.float32
        )
        / TOKENS
    )
    parts = local_term.reshape(-1, 2, 8, rank)
    keep = lax.dynamic_index_in_dim(parts, core, 1, keepdims=False)
    send = lax.dynamic_index_in_dim(parts, 1 - core, 1, keepdims=False).astype(jnp.bfloat16)
    sent = lax.all_gather(send, "c", axis=0)
    received = lax.dynamic_index_in_dim(sent, 1 - core, 0, keepdims=False)
    chip_term = keep + received.astype(jnp.float32)
    low_grad = exchange_sum(chip_term.reshape(-1, rank), ("zl", "y"))
    new_first = first_decay * first_moment + (1.0 - first_decay) * low_grad
    new_second = second_decay * second_moment + (1.0 - second_decay) * low_grad * low_grad
    update = (new_first / first_fix / (jnp.sqrt(new_second / second_fix) + tiny_eps)).astype(
        jnp.bfloat16
    )
    update, basis_pieces = lax.optimization_barrier((update, basis_pieces))
    updates = lax.all_gather(gather(update, ("zl", "y")), "c", axis=0)
    return (decode(updates, basis_pieces, weight), new_first, new_second)


def solution(mesh):
    named = Mesh(mesh.devices.reshape(SIZES), AXES)
    return jax.shard_map(
        local,
        mesh=named,
        in_specs=(
            P(DP, FSDP),
            P(DP, FSDP),
            P(FSDP, None),
            P(FSDP, None),
            P(FSDP + DP, None),
            P(FSDP + DP, None),
        ),
        out_specs=(P(FSDP, None), P(FSDP + DP, None), P(FSDP + DP, None)),
        check_vma=False,
    )
```

```python
import jax
import jax.numpy as jnp
from jax import lax
from jax.experimental import pallas as pl
from jax.experimental.pallas import tpu as pltpu
from jax.sharding import Mesh
from jax.sharding import PartitionSpec as P

first_decay = 0.9
second_decay = 0.999
first_fix = 1.0 - 0.9**10
second_fix = 1.0 - 0.999**10
step_rate = 0.01
tiny_eps = 1e-08

AXES = ("zl", "y", "c", "zh", "x")
SIZES = (4, 4, 2, 4, 4)
DP = ("zl", "y", "c")
FSDP = ("zh", "x")
TOKENS = 8192


def exchange_sum(value, axis):
    size = lax.axis_size(axis)
    rows, cols = value.shape
    parts = value.astype(jnp.bfloat16).reshape(size, rows // size, cols)
    parts = lax.all_to_all(parts, axis, 0, 0, tiled=True)
    return jnp.sum(parts.astype(jnp.float32), axis=0)


def gather(value, axis):
    size = lax.axis_size(axis)
    copies = jnp.broadcast_to(value[None], (size,) + value.shape)
    return lax.all_to_all(copies, axis, 0, 0, tiled=True).reshape(
        size * value.shape[0], value.shape[1]
    )


STEP = 2


def decode_kernel(update_ref, basis_ref, weight_ref, out_ref, new, sems):
    two, ys, xs, zhs, piece, rank = basis_ref.shape
    shard = two * ys * piece
    cols = STEP * shard

    def copy_out(i):
        where = pl.ds(i * cols, cols)
        return pltpu.make_async_copy(new.at[:, where], out_ref.at[:, where], sems.at[i])

    updates = update_ref[...].reshape(-1, rank)
    steps = xs * zhs // STEP
    for i in range(steps):
        shards = [
            basis_ref[:, :, f % xs, f // xs].reshape(shard, rank)
            for f in range(i * STEP, (i + 1) * STEP)
        ]
        decoded = lax.dot_general(
            updates,
            jnp.concatenate(shards, axis=0),
            (((1,), (1,)), ((), ())),
            preferred_element_type=jnp.float32,
        )
        decoded = decoded.reshape(2, -1, 8, cols)
        decoded = jnp.stack([decoded[0], decoded[1]], axis=1).reshape(-1, cols)
        old = weight_ref[:, i * cols : (i + 1) * cols].astype(jnp.float32)
        new[:, i * cols : (i + 1) * cols] = (old - step_rate * decoded).astype(new.dtype)
        copy_out(i).start()
    for i in range(steps):
        copy_out(i).wait()


def decode(updates, basis_pieces, weight):
    steps = basis_pieces.shape[2] * basis_pieces.shape[3] // STEP
    return pl.pallas_call(
        decode_kernel,
        in_specs=[pl.BlockSpec(memory_space=pltpu.VMEM)] * 3,
        out_specs=pl.BlockSpec(memory_space=pl.ANY),
        out_shape=jax.ShapeDtypeStruct(weight.shape, weight.dtype),
        scratch_shapes=[
            pltpu.VMEM(weight.shape, weight.dtype),
            pltpu.SemaphoreType.DMA((steps,)),
        ],
        compiler_params=pltpu.CompilerParams(vmem_limit_bytes=24 * 1024 * 1024),
        name="decode",
    )(updates, basis_pieces, weight)


def local(activations, output_grads, basis, weight, first_moment, second_moment):
    core = lax.axis_index("c")
    partial_product = jnp.dot(activations, basis, preferred_element_type=jnp.float32)
    over_x = exchange_sum(partial_product, "x").astype(jnp.bfloat16)
    rank = over_x.shape[1]

    piece = basis.shape[0] // 8
    mine = lax.dynamic_slice_in_dim(basis, (core * 4 + lax.axis_index("y")) * piece, piece, 0)
    over_x, mine = lax.optimization_barrier((over_x, mine))
    mine = lax.all_gather(mine, "zh", axis=0, tiled=True)
    over_x, mine = lax.optimization_barrier((over_x, mine))
    basis_pieces = lax.all_gather(mine, ("c", "y", "x"), axis=0, tiled=True)
    basis_pieces = basis_pieces.reshape(2, 4, 4, 4, piece, rank)

    over_all = lax.all_gather(over_x, "zh", axis=0)
    block = jnp.sum(over_all.astype(jnp.float32), axis=0).astype(jnp.bfloat16)
    projected = gather(block, "x")
    local_term = (
        lax.dot_general(
            output_grads, projected, (((0,), (0,)), ((), ())), preferred_element_type=jnp.float32
        )
        / TOKENS
    )
    parts = local_term.reshape(-1, 2, 8, rank)
    keep = lax.dynamic_index_in_dim(parts, core, 1, keepdims=False)
    send = lax.dynamic_index_in_dim(parts, 1 - core, 1, keepdims=False).astype(jnp.bfloat16)
    sent = lax.all_gather(send, "c", axis=0)
    received = lax.dynamic_index_in_dim(sent, 1 - core, 0, keepdims=False)
    chip_term = keep + received.astype(jnp.float32)
    low_grad = exchange_sum(chip_term.reshape(-1, rank), ("zl", "y"))
    new_first = first_decay * first_moment + (1.0 - first_decay) * low_grad
    new_second = second_decay * second_moment + (1.0 - second_decay) * low_grad * low_grad
    update = (new_first / first_fix / (jnp.sqrt(new_second / second_fix) + tiny_eps)).astype(
        jnp.bfloat16
    )
    updates = lax.all_gather(gather(update, ("zl", "y")), "c", axis=0)
    return (decode(updates, basis_pieces, weight), new_first, new_second)


def solution(mesh):
    named = Mesh(mesh.devices.reshape(SIZES), AXES)
    return jax.shard_map(
        local,
        mesh=named,
        in_specs=(
            P(DP, FSDP),
            P(DP, FSDP),
            P(FSDP, None),
            P(FSDP, None),
            P(FSDP + DP, None),
            P(FSDP + DP, None),
        ),
        out_specs=(P(FSDP, None), P(FSDP + DP, None), P(FSDP + DP, None)),
        check_vma=False,
    )
```

```python
import jax
import jax.numpy as jnp
from jax import lax
from jax.experimental import pallas as pl
from jax.experimental.pallas import tpu as pltpu
from jax.sharding import Mesh
from jax.sharding import PartitionSpec as P

first_decay = 0.9
second_decay = 0.999
first_fix = 1.0 - 0.9**10
second_fix = 1.0 - 0.999**10
step_rate = 0.01
tiny_eps = 1e-08

AXES = ("zl", "y", "c", "zh", "x")
SIZES = (4, 4, 2, 4, 4)
DP = ("zl", "y", "c")
FSDP = ("zh", "x")
TOKENS = 8192


def exchange_sum(value, axis):
    size = lax.axis_size(axis)
    rows, cols = value.shape
    parts = value.astype(jnp.bfloat16).reshape(size, rows // size, cols)
    parts = lax.all_to_all(parts, axis, 0, 0, tiled=True)
    return jnp.sum(parts.astype(jnp.float32), axis=0)


def gather(value, axis):
    size = lax.axis_size(axis)
    copies = jnp.broadcast_to(value[None], (size,) + value.shape)
    return lax.all_to_all(copies, axis, 0, 0, tiled=True).reshape(
        size * value.shape[0], value.shape[1]
    )


STEP = 2


def decode_kernel(update_ref, basis_ref, weight_ref, out_ref, new, sems):
    two, ys, xs, zhs, piece, rank = basis_ref.shape
    shard = two * ys * piece
    cols = STEP * shard

    def copy_out(i):
        where = pl.ds(i * cols, cols)
        return pltpu.make_async_copy(new.at[:, where], out_ref.at[:, where], sems.at[i])

    updates = update_ref[...].reshape(-1, rank)
    steps = xs * zhs // STEP
    for i in range(steps):
        shards = [
            basis_ref[:, :, f % xs, f // xs].reshape(shard, rank)
            for f in range(i * STEP, (i + 1) * STEP)
        ]
        decoded = lax.dot_general(
            updates,
            jnp.concatenate(shards, axis=0),
            (((1,), (1,)), ((), ())),
            preferred_element_type=jnp.float32,
        )
        decoded = decoded.reshape(2, -1, 8, cols)
        decoded = jnp.stack([decoded[0], decoded[1]], axis=1).reshape(-1, cols)
        old = weight_ref[:, i * cols : (i + 1) * cols].astype(jnp.float32)
        new[:, i * cols : (i + 1) * cols] = (old - step_rate * decoded).astype(new.dtype)
        copy_out(i).start()
    for i in range(steps):
        copy_out(i).wait()


def decode(updates, basis_pieces, weight):
    steps = basis_pieces.shape[2] * basis_pieces.shape[3] // STEP
    return pl.pallas_call(
        decode_kernel,
        in_specs=[pl.BlockSpec(memory_space=pltpu.VMEM)] * 3,
        out_specs=pl.BlockSpec(memory_space=pl.ANY),
        out_shape=jax.ShapeDtypeStruct(weight.shape, weight.dtype),
        scratch_shapes=[
            pltpu.VMEM(weight.shape, weight.dtype),
            pltpu.SemaphoreType.DMA((steps,)),
        ],
        compiler_params=pltpu.CompilerParams(vmem_limit_bytes=24 * 1024 * 1024),
        name="decode",
    )(updates, basis_pieces, weight)


def local(activations, output_grads, basis, weight, first_moment, second_moment):
    core = lax.axis_index("c")
    partial_product = jnp.dot(activations, basis, preferred_element_type=jnp.float32)
    piece = basis.shape[0] // 8
    mine = lax.dynamic_slice_in_dim(basis, (core * 4 + lax.axis_index("y")) * piece, piece, 0)
    partial_product, mine = lax.optimization_barrier((partial_product.astype(jnp.bfloat16), mine))
    over_x = exchange_sum(partial_product, "x").astype(jnp.bfloat16)
    rank = over_x.shape[1]
    mine = lax.all_gather(mine, "zh", axis=0, tiled=True)
    over_x, mine = lax.optimization_barrier((over_x, mine))
    basis_pieces = lax.all_gather(mine, ("c", "y", "x"), axis=0, tiled=True)
    basis_pieces = basis_pieces.reshape(2, 4, 4, 4, piece, rank)

    over_all = lax.all_gather(over_x, "zh", axis=0)
    block = jnp.sum(over_all.astype(jnp.float32), axis=0).astype(jnp.bfloat16)
    projected = gather(block, "x")
    local_term = (
        lax.dot_general(
            output_grads, projected, (((0,), (0,)), ((), ())), preferred_element_type=jnp.float32
        )
        / TOKENS
    )
    parts = local_term.reshape(-1, 2, 8, rank)
    keep = lax.dynamic_index_in_dim(parts, core, 1, keepdims=False)
    send = lax.dynamic_index_in_dim(parts, 1 - core, 1, keepdims=False).astype(jnp.bfloat16)
    sent = lax.all_gather(send, "c", axis=0)
    received = lax.dynamic_index_in_dim(sent, 1 - core, 0, keepdims=False)
    chip_term = keep + received.astype(jnp.float32)
    low_grad = exchange_sum(chip_term.reshape(-1, rank), ("zl", "y"))
    new_first = first_decay * first_moment + (1.0 - first_decay) * low_grad
    new_second = second_decay * second_moment + (1.0 - second_decay) * low_grad * low_grad
    update = (new_first / first_fix / (jnp.sqrt(new_second / second_fix) + tiny_eps)).astype(
        jnp.bfloat16
    )
    updates = lax.all_gather(gather(update, ("zl", "y")), "c", axis=0)
    return (decode(updates, basis_pieces, weight), new_first, new_second)


def solution(mesh):
    named = Mesh(mesh.devices.reshape(SIZES), AXES)
    return jax.shard_map(
        local,
        mesh=named,
        in_specs=(
            P(DP, FSDP),
            P(DP, FSDP),
            P(FSDP, None),
            P(FSDP, None),
            P(FSDP + DP, None),
            P(FSDP + DP, None),
        ),
        out_specs=(P(FSDP, None), P(FSDP + DP, None), P(FSDP + DP, None)),
        check_vma=False,
    )
```

```python
import jax
import jax.numpy as jnp
from jax import lax
from jax.experimental import pallas as pl
from jax.experimental.pallas import tpu as pltpu
from jax.sharding import Mesh
from jax.sharding import PartitionSpec as P

first_decay = 0.9
second_decay = 0.999
first_fix = 1.0 - 0.9**10
second_fix = 1.0 - 0.999**10
step_rate = 0.01
tiny_eps = 1e-08

AXES = ("zl", "y", "c", "zh", "x")
SIZES = (4, 4, 2, 4, 4)
DP = ("zl", "y", "c")
FSDP = ("zh", "x")
TOKENS = 8192


def exchange_sum(value, axis):
    size = lax.axis_size(axis)
    rows, cols = value.shape
    parts = value.astype(jnp.bfloat16).reshape(size, rows // size, cols)
    parts = lax.all_to_all(parts, axis, 0, 0, tiled=True)
    return jnp.sum(parts.astype(jnp.float32), axis=0)


def gather(value, axis):
    size = lax.axis_size(axis)
    copies = jnp.broadcast_to(value[None], (size,) + value.shape)
    return lax.all_to_all(copies, axis, 0, 0, tiled=True).reshape(
        size * value.shape[0], value.shape[1]
    )


STEP = 2


def decode_kernel(core_ref, update_ref, mine_ref, other_ref, weight_ref, out_ref, new, sems):
    ys, xs, zhs, piece, rank = mine_ref.shape
    half = ys * piece
    cols = STEP * 2 * half
    first = core_ref[0] == 0

    def copy_out(i):
        where = pl.ds(i * cols, cols)
        return pltpu.make_async_copy(new.at[:, where], out_ref.at[:, where], sems.at[i])

    updates = update_ref[...].reshape(-1, rank)
    steps = xs * zhs // STEP
    for i in range(steps):
        halves = [
            ref[:, f % xs, f // xs].reshape(half, rank)
            for f in range(i * STEP, (i + 1) * STEP)
            for ref in (mine_ref, other_ref)
        ]
        decoded = lax.dot_general(
            updates,
            jnp.concatenate(halves, axis=0),
            (((1,), (1,)), ((), ())),
            preferred_element_type=jnp.float32,
        )
        decoded = decoded.reshape(2, -1, 8, cols)
        decoded = jnp.stack([decoded[0], decoded[1]], axis=1).reshape(-1, cols)
        for k in range(0, 2 * STEP, 2):
            own = decoded[:, k * half : (k + 1) * half]
            other = decoded[:, (k + 1) * half : (k + 2) * half]
            for j, part in ((k, jnp.where(first, own, other)), (k + 1, jnp.where(first, other, own))):
                at = slice(i * cols + j * half, i * cols + (j + 1) * half)
                old = weight_ref[:, at].astype(jnp.float32)
                new[:, at] = (old - step_rate * part).astype(new.dtype)
        copy_out(i).start()
    for i in range(steps):
        copy_out(i).wait()


def decode(core, updates, mine, other, weight):
    steps = mine.shape[1] * mine.shape[2] // STEP
    vmem = pl.BlockSpec(memory_space=pltpu.VMEM)
    return pl.pallas_call(
        decode_kernel,
        in_specs=[pl.BlockSpec(memory_space=pltpu.SMEM), vmem, vmem, vmem, vmem],
        out_specs=pl.BlockSpec(memory_space=pl.ANY),
        out_shape=jax.ShapeDtypeStruct(weight.shape, weight.dtype),
        scratch_shapes=[
            pltpu.VMEM(weight.shape, weight.dtype),
            pltpu.SemaphoreType.DMA((steps,)),
        ],
        compiler_params=pltpu.CompilerParams(vmem_limit_bytes=24 * 1024 * 1024),
        name="decode",
    )(core, updates, mine, other, weight)


def local(activations, output_grads, basis, weight, first_moment, second_moment):
    core = lax.axis_index("c")
    partial_product = jnp.dot(activations, basis, preferred_element_type=jnp.float32)
    piece = basis.shape[0] // 8
    mine = lax.dynamic_slice_in_dim(basis, (core * 4 + lax.axis_index("y")) * piece, piece, 0)
    partial_product, mine = lax.optimization_barrier((partial_product.astype(jnp.bfloat16), mine))
    over_x = exchange_sum(partial_product, "x").astype(jnp.bfloat16)
    rank = over_x.shape[1]
    mine = lax.all_gather(mine, "zh", axis=0, tiled=True)
    over_x, mine = lax.optimization_barrier((over_x, mine))
    basis_half = gather(mine, ("y", "x"))

    over_all = lax.all_gather(over_x, "zh", axis=0)
    block = jnp.sum(over_all.astype(jnp.float32), axis=0).astype(jnp.bfloat16)
    projected = lax.all_gather(block, "x", axis=0, tiled=True)
    local_term = (
        lax.dot_general(
            output_grads, projected, (((0,), (0,)), ((), ())), preferred_element_type=jnp.float32
        )
        / TOKENS
    )
    parts = local_term.reshape(-1, 2, 8, rank)
    keep = lax.dynamic_index_in_dim(parts, core, 1, keepdims=False)
    send = lax.dynamic_index_in_dim(parts, 1 - core, 1, keepdims=False).astype(jnp.bfloat16)
    sent = lax.all_gather(send, "c", axis=0)
    received = lax.dynamic_index_in_dim(sent, 1 - core, 0, keepdims=False)
    chip_term = keep + received.astype(jnp.float32)
    chip_term, basis_half = lax.optimization_barrier((chip_term, basis_half))
    other_half = lax.ppermute(basis_half, "c", [(0, 1), (1, 0)])
    low_grad = exchange_sum(chip_term.reshape(-1, rank), ("zl", "y"))
    new_first = first_decay * first_moment + (1.0 - first_decay) * low_grad
    new_second = second_decay * second_moment + (1.0 - second_decay) * low_grad * low_grad
    update = (new_first / first_fix / (jnp.sqrt(new_second / second_fix) + tiny_eps)).astype(
        jnp.bfloat16
    )
    updates = lax.all_gather(gather(update, ("zl", "y")), "c", axis=0)
    which = jnp.full((1,), core, jnp.int32)
    shape = (4, 4, 4, piece, rank)
    new_weight = decode(
        which, updates, basis_half.reshape(shape), other_half.reshape(shape), weight
    )
    return (new_weight, new_first, new_second)


def solution(mesh):
    named = Mesh(mesh.devices.reshape(SIZES), AXES)
    return jax.shard_map(
        local,
        mesh=named,
        in_specs=(
            P(DP, FSDP),
            P(DP, FSDP),
            P(FSDP, None),
            P(FSDP, None),
            P(FSDP + DP, None),
            P(FSDP + DP, None),
        ),
        out_specs=(P(FSDP, None), P(FSDP + DP, None), P(FSDP + DP, None)),
        check_vma=False,
    )
```

```python
import jax
import jax.numpy as jnp
from jax import lax
from jax.experimental import pallas as pl
from jax.experimental.pallas import tpu as pltpu
from jax.sharding import Mesh
from jax.sharding import PartitionSpec as P

first_decay = 0.9
second_decay = 0.999
first_fix = 1.0 - 0.9**10
second_fix = 1.0 - 0.999**10
step_rate = 0.01
tiny_eps = 1e-08

AXES = ("zl", "y", "c", "zh", "x")
SIZES = (4, 4, 2, 4, 4)
DP = ("zl", "y", "c")
FSDP = ("zh", "x")
TOKENS = 8192


def exchange_sum(value, axis):
    size = lax.axis_size(axis)
    rows, cols = value.shape
    parts = value.astype(jnp.bfloat16).reshape(size, rows // size, cols)
    parts = lax.all_to_all(parts, axis, 0, 0, tiled=True)
    return jnp.sum(parts.astype(jnp.float32), axis=0)


def gather(value, axis):
    size = lax.axis_size(axis)
    copies = jnp.broadcast_to(value[None], (size,) + value.shape)
    return lax.all_to_all(copies, axis, 0, 0, tiled=True).reshape(
        size * value.shape[0], value.shape[1]
    )


def product_kernel(left_ref, right_ref, out_ref, left, right, out, sems):
    copies = [
        pltpu.make_async_copy(left_ref, left, sems.at[0]),
        pltpu.make_async_copy(right_ref, right, sems.at[1]),
    ]
    for copy in copies:
        copy.start()
    for copy in copies:
        copy.wait()
    out[...] = jnp.dot(left[...], right[...], preferred_element_type=jnp.float32).astype(out.dtype)
    store = pltpu.make_async_copy(out, out_ref, sems.at[2])
    store.start()
    store.wait()


def product(left, right):
    shape = (left.shape[0], right.shape[1])
    return pl.pallas_call(
        product_kernel,
        in_specs=[pl.BlockSpec(memory_space=pl.ANY)] * 2,
        out_specs=pl.BlockSpec(memory_space=pl.ANY),
        out_shape=jax.ShapeDtypeStruct(shape, jnp.bfloat16),
        scratch_shapes=[
            pltpu.VMEM(left.shape, left.dtype),
            pltpu.VMEM(right.shape, right.dtype),
            pltpu.VMEM(shape, jnp.bfloat16),
            pltpu.SemaphoreType.DMA((3,)),
        ],
        compiler_params=pltpu.CompilerParams(vmem_limit_bytes=60 * 1024 * 1024),
        name="product",
    )(left, right)


STEP = 2


def decode_kernel(update_ref, basis_ref, weight_ref, out_ref, new, sems):
    two, ys, xs, zhs, piece, rank = basis_ref.shape
    shard = two * ys * piece
    cols = STEP * shard

    def copy_out(i):
        where = pl.ds(i * cols, cols)
        return pltpu.make_async_copy(new.at[:, where], out_ref.at[:, where], sems.at[i])

    updates = update_ref[...].reshape(-1, rank)
    steps = xs * zhs // STEP
    for i in range(steps):
        shards = [
            basis_ref[:, :, f % xs, f // xs].reshape(shard, rank)
            for f in range(i * STEP, (i + 1) * STEP)
        ]
        decoded = lax.dot_general(
            updates,
            jnp.concatenate(shards, axis=0),
            (((1,), (1,)), ((), ())),
            preferred_element_type=jnp.float32,
        )
        decoded = decoded.reshape(2, -1, 8, cols)
        decoded = jnp.stack([decoded[0], decoded[1]], axis=1).reshape(-1, cols)
        old = weight_ref[:, i * cols : (i + 1) * cols].astype(jnp.float32)
        new[:, i * cols : (i + 1) * cols] = (old - step_rate * decoded).astype(new.dtype)
        copy_out(i).start()
    for i in range(steps):
        copy_out(i).wait()


def decode(updates, basis_pieces, weight):
    steps = basis_pieces.shape[2] * basis_pieces.shape[3] // STEP
    return pl.pallas_call(
        decode_kernel,
        in_specs=[pl.BlockSpec(memory_space=pltpu.VMEM)] * 3,
        out_specs=pl.BlockSpec(memory_space=pl.ANY),
        out_shape=jax.ShapeDtypeStruct(weight.shape, weight.dtype),
        scratch_shapes=[
            pltpu.VMEM(weight.shape, weight.dtype),
            pltpu.SemaphoreType.DMA((steps,)),
        ],
        compiler_params=pltpu.CompilerParams(vmem_limit_bytes=24 * 1024 * 1024),
        name="decode",
    )(updates, basis_pieces, weight)


def local(activations, output_grads, basis, weight, first_moment, second_moment):
    core = lax.axis_index("c")
    partial_product = product(activations, basis)
    piece = basis.shape[0] // 8
    mine = lax.dynamic_slice_in_dim(basis, (core * 4 + lax.axis_index("y")) * piece, piece, 0)
    partial_product, mine, first = lax.optimization_barrier((partial_product, mine, core == 0))
    over_x = exchange_sum(partial_product, "x").astype(jnp.bfloat16)
    rank = over_x.shape[1]
    mine = lax.all_gather(mine, "zh", axis=0, tiled=True)
    over_x, mine = lax.optimization_barrier((over_x, mine))
    basis_pieces = lax.all_gather(mine, ("c", "y", "x"), axis=0, tiled=True)
    basis_pieces = basis_pieces.reshape(2, 4, 4, 4, piece, rank)

    over_all = lax.all_gather(over_x, "zh", axis=0)
    block = jnp.sum(over_all.astype(jnp.float32), axis=0).astype(jnp.bfloat16)
    projected = gather(block, "x")
    local_term = (
        lax.dot_general(
            output_grads, projected, (((0,), (0,)), ((), ())), preferred_element_type=jnp.float32
        )
        / TOKENS
    )
    parts = local_term.reshape(-1, 2, 8, rank)
    keep = jnp.where(first, parts[:, 0], parts[:, 1])
    send = jnp.where(first, parts[:, 1], parts[:, 0]).astype(jnp.bfloat16)
    sent = lax.all_gather(send, "c", axis=0)
    received = jnp.where(first, sent[1], sent[0])
    chip_term = keep + received.astype(jnp.float32)
    low_grad = exchange_sum(chip_term.reshape(-1, rank), ("zl", "y"))
    new_first = first_decay * first_moment + (1.0 - first_decay) * low_grad
    new_second = second_decay * second_moment + (1.0 - second_decay) * low_grad * low_grad
    update = (new_first / first_fix / (jnp.sqrt(new_second / second_fix) + tiny_eps)).astype(
        jnp.bfloat16
    )
    updates = lax.all_gather(gather(update, ("zl", "y")), "c", axis=0)
    return (decode(updates, basis_pieces, weight), new_first, new_second)


def solution(mesh):
    named = Mesh(mesh.devices.reshape(SIZES), AXES)
    return jax.shard_map(
        local,
        mesh=named,
        in_specs=(
            P(DP, FSDP),
            P(DP, FSDP),
            P(FSDP, None),
            P(FSDP, None),
            P(FSDP + DP, None),
            P(FSDP + DP, None),
        ),
        out_specs=(P(FSDP, None), P(FSDP + DP, None), P(FSDP + DP, None)),
        check_vma=False,
    )
```

```python
import jax
import jax.numpy as jnp
from jax import lax
from jax.experimental import pallas as pl
from jax.experimental.pallas import tpu as pltpu
from jax.sharding import Mesh
from jax.sharding import PartitionSpec as P

first_decay = 0.9
second_decay = 0.999
first_fix = 1.0 - 0.9**10
second_fix = 1.0 - 0.999**10
step_rate = 0.01
tiny_eps = 1e-08

AXES = ("zl", "y", "c", "zh", "x")
SIZES = (4, 4, 2, 4, 4)
DP = ("zl", "y", "c")
FSDP = ("zh", "x")
TOKENS = 8192


def exchange_sum(value, axis):
    size = lax.axis_size(axis)
    rows, cols = value.shape
    parts = value.astype(jnp.bfloat16).reshape(size, rows // size, cols)
    parts = lax.all_to_all(parts, axis, 0, 0, tiled=True)
    return jnp.sum(parts.astype(jnp.float32), axis=0)


def gather(value, axis):
    size = lax.axis_size(axis)
    copies = jnp.broadcast_to(value[None], (size,) + value.shape)
    return lax.all_to_all(copies, axis, 0, 0, tiled=True).reshape(
        size * value.shape[0], value.shape[1]
    )


def product_kernel(start_ref, left_ref, right_ref, out_ref, piece_ref, left, right, out, sems):
    rows = piece_ref.shape[0]
    loads = [
        pltpu.make_async_copy(right_ref, right, sems.at[0]),
        pltpu.make_async_copy(left_ref, left, sems.at[1]),
    ]
    for load in loads:
        load.start()
    for load in loads:
        load.wait()
    where = pl.ds(pl.multiple_of(start_ref[0] * rows, rows), rows)
    piece = pltpu.make_async_copy(right.at[where], piece_ref, sems.at[2])
    piece.start()
    out[...] = jnp.dot(left[...], right[...], preferred_element_type=jnp.float32).astype(out.dtype)
    store = pltpu.make_async_copy(out, out_ref, sems.at[3])
    store.start()
    piece.wait()
    store.wait()


def product(left, right, which, rows):
    shape = (left.shape[0], right.shape[1])
    anywhere = pl.BlockSpec(memory_space=pl.ANY)
    return pl.pallas_call(
        product_kernel,
        in_specs=[pl.BlockSpec(memory_space=pltpu.SMEM), anywhere, anywhere],
        out_specs=[anywhere, anywhere],
        out_shape=[
            jax.ShapeDtypeStruct(shape, jnp.bfloat16),
            jax.ShapeDtypeStruct((rows, right.shape[1]), right.dtype),
        ],
        scratch_shapes=[
            pltpu.VMEM(left.shape, left.dtype),
            pltpu.VMEM(right.shape, right.dtype),
            pltpu.VMEM(shape, jnp.bfloat16),
            pltpu.SemaphoreType.DMA((4,)),
        ],
        compiler_params=pltpu.CompilerParams(vmem_limit_bytes=60 * 1024 * 1024),
        name="product",
    )(which, left, right)


STEP = 2


def decode_kernel(update_ref, basis_ref, weight_ref, out_ref, new, sems):
    two, ys, xs, zhs, piece, rank = basis_ref.shape
    shard = two * ys * piece
    cols = STEP * shard

    def copy_out(i):
        where = pl.ds(i * cols, cols)
        return pltpu.make_async_copy(new.at[:, where], out_ref.at[:, where], sems.at[i])

    updates = update_ref[...].reshape(-1, rank)
    steps = xs * zhs // STEP
    for i in range(steps):
        shards = [
            basis_ref[:, :, f % xs, f // xs].reshape(shard, rank)
            for f in range(i * STEP, (i + 1) * STEP)
        ]
        decoded = lax.dot_general(
            updates,
            jnp.concatenate(shards, axis=0),
            (((1,), (1,)), ((), ())),
            preferred_element_type=jnp.float32,
        )
        decoded = decoded.reshape(2, -1, 8, cols)
        decoded = jnp.stack([decoded[0], decoded[1]], axis=1).reshape(-1, cols)
        old = weight_ref[:, i * cols : (i + 1) * cols].astype(jnp.float32)
        new[:, i * cols : (i + 1) * cols] = (old - step_rate * decoded).astype(new.dtype)
        copy_out(i).start()
    for i in range(steps):
        copy_out(i).wait()


def decode(updates, basis_pieces, weight):
    steps = basis_pieces.shape[2] * basis_pieces.shape[3] // STEP
    return pl.pallas_call(
        decode_kernel,
        in_specs=[pl.BlockSpec(memory_space=pltpu.VMEM)] * 3,
        out_specs=pl.BlockSpec(memory_space=pl.ANY),
        out_shape=jax.ShapeDtypeStruct(weight.shape, weight.dtype),
        scratch_shapes=[
            pltpu.VMEM(weight.shape, weight.dtype),
            pltpu.SemaphoreType.DMA((steps,)),
        ],
        compiler_params=pltpu.CompilerParams(vmem_limit_bytes=24 * 1024 * 1024),
        name="decode",
    )(updates, basis_pieces, weight)


def local(activations, output_grads, basis, weight, first_moment, second_moment):
    core = lax.axis_index("c")
    piece = basis.shape[0] // 8
    which = jnp.full((1,), core * 4 + lax.axis_index("y"), jnp.int32)
    partial_product, mine = product(activations, basis, which, piece)
    partial_product, mine, first = lax.optimization_barrier((partial_product, mine, core == 0))
    rows, rank = partial_product.shape
    blocks = lax.all_to_all(
        partial_product.reshape(4, rows // 4, rank), "x", 0, 0, tiled=True
    )
    mine = lax.all_gather(mine, "zh", axis=0, tiled=True)
    blocks, mine = lax.optimization_barrier((blocks, mine))
    over_x = jnp.sum(blocks.astype(jnp.float32), axis=0).astype(jnp.bfloat16)
    basis_pieces = lax.all_gather(mine, ("c", "y", "x"), axis=0, tiled=True)
    basis_pieces = basis_pieces.reshape(2, 4, 4, 4, piece, rank)

    over_all = lax.all_gather(over_x, "zh", axis=0)
    block = jnp.sum(over_all.astype(jnp.float32), axis=0).astype(jnp.bfloat16)
    projected = gather(block, "x")
    local_term = (
        lax.dot_general(
            output_grads, projected, (((0,), (0,)), ((), ())), preferred_element_type=jnp.float32
        )
        / TOKENS
    )
    parts = local_term.reshape(-1, 2, 8, rank)
    keep = jnp.where(first, parts[:, 0], parts[:, 1])
    send = jnp.where(first, parts[:, 1], parts[:, 0]).astype(jnp.bfloat16)
    sent = lax.all_gather(send, "c", axis=0)
    received = jnp.where(first, sent[1], sent[0])
    chip_term = keep + received.astype(jnp.float32)
    low_grad = exchange_sum(chip_term.reshape(-1, rank), ("zl", "y"))
    new_first = first_decay * first_moment + (1.0 - first_decay) * low_grad
    new_second = second_decay * second_moment + (1.0 - second_decay) * low_grad * low_grad
    update = (new_first / first_fix / (jnp.sqrt(new_second / second_fix) + tiny_eps)).astype(
        jnp.bfloat16
    )
    updates = lax.all_gather(gather(update, ("zl", "y")), "c", axis=0)
    return (decode(updates, basis_pieces, weight), new_first, new_second)


def solution(mesh):
    named = Mesh(mesh.devices.reshape(SIZES), AXES)
    return jax.shard_map(
        local,
        mesh=named,
        in_specs=(
            P(DP, FSDP),
            P(DP, FSDP),
            P(FSDP, None),
            P(FSDP, None),
            P(FSDP + DP, None),
            P(FSDP + DP, None),
        ),
        out_specs=(P(FSDP, None), P(FSDP + DP, None), P(FSDP + DP, None)),
        check_vma=False,
    )
```

```python
import jax
import jax.numpy as jnp
from jax import lax
from jax.experimental import pallas as pl
from jax.experimental.pallas import tpu as pltpu
from jax.sharding import Mesh
from jax.sharding import PartitionSpec as P

first_decay = 0.9
second_decay = 0.999
first_fix = 1.0 - 0.9**10
second_fix = 1.0 - 0.999**10
step_rate = 0.01
tiny_eps = 1e-08

AXES = ("zl", "y", "c", "zh", "x")
SIZES = (4, 4, 2, 4, 4)
DP = ("zl", "y", "c")
FSDP = ("zh", "x")
TOKENS = 8192


def exchange_sum(value, axis):
    size = lax.axis_size(axis)
    rows, cols = value.shape
    parts = value.astype(jnp.bfloat16).reshape(size, rows // size, cols)
    parts = lax.all_to_all(parts, axis, 0, 0, tiled=True)
    return jnp.sum(parts.astype(jnp.float32), axis=0)


def gather(value, axis):
    size = lax.axis_size(axis)
    copies = jnp.broadcast_to(value[None], (size,) + value.shape)
    return lax.all_to_all(copies, axis, 0, 0, tiled=True).reshape(
        size * value.shape[0], value.shape[1]
    )


def product_kernel(start_ref, left_ref, right_ref, out_ref, piece_ref, left, right, out, sems):
    rows = piece_ref.shape[0]
    loads = [
        pltpu.make_async_copy(right_ref, right, sems.at[0]),
        pltpu.make_async_copy(left_ref, left, sems.at[1]),
    ]
    for load in loads:
        load.start()
    for load in loads:
        load.wait()
    where = pl.ds(pl.multiple_of(start_ref[0] * rows, rows), rows)
    piece = pltpu.make_async_copy(right.at[where], piece_ref, sems.at[2])
    piece.start()
    out[...] = jnp.dot(left[...], right[...], preferred_element_type=jnp.float32).astype(out.dtype)
    store = pltpu.make_async_copy(out, out_ref, sems.at[3])
    store.start()
    piece.wait()
    store.wait()


def product(left, right, which, rows):
    shape = (left.shape[0], right.shape[1])
    anywhere = pl.BlockSpec(memory_space=pl.ANY)
    return pl.pallas_call(
        product_kernel,
        in_specs=[pl.BlockSpec(memory_space=pltpu.SMEM), anywhere, anywhere],
        out_specs=[anywhere, anywhere],
        out_shape=[
            jax.ShapeDtypeStruct(shape, jnp.bfloat16),
            jax.ShapeDtypeStruct((rows, right.shape[1]), right.dtype),
        ],
        scratch_shapes=[
            pltpu.VMEM(left.shape, left.dtype),
            pltpu.VMEM(right.shape, right.dtype),
            pltpu.VMEM(shape, jnp.bfloat16),
            pltpu.SemaphoreType.DMA((4,)),
        ],
        compiler_params=pltpu.CompilerParams(vmem_limit_bytes=60 * 1024 * 1024),
        name="product",
    )(which, left, right)


STEP = 2


def decode_kernel(update_ref, basis_ref, weight_ref, out_ref, new, sems):
    ys, xs, two, zhs, piece, rank = basis_ref.shape
    shard = two * ys * piece
    cols = STEP * shard

    def copy_out(i):
        where = pl.ds(i * cols, cols)
        return pltpu.make_async_copy(new.at[:, where], out_ref.at[:, where], sems.at[i])

    updates = update_ref[...].reshape(-1, rank)
    steps = xs * zhs // STEP
    for i in range(steps):
        shards = [
            basis_ref[:, f % xs, :, f // xs].reshape(shard, rank)
            for f in range(i * STEP, (i + 1) * STEP)
        ]
        decoded = lax.dot_general(
            updates,
            jnp.concatenate(shards, axis=0),
            (((1,), (1,)), ((), ())),
            preferred_element_type=jnp.float32,
        )
        decoded = decoded.reshape(2, -1, 8, cols)
        decoded = jnp.stack([decoded[0], decoded[1]], axis=1).reshape(-1, cols)
        old = weight_ref[:, i * cols : (i + 1) * cols].astype(jnp.float32)
        new[:, i * cols : (i + 1) * cols] = (old - step_rate * decoded).astype(new.dtype)
        copy_out(i).start()
    for i in range(steps):
        copy_out(i).wait()


def decode(updates, basis_pieces, weight):
    steps = basis_pieces.shape[1] * basis_pieces.shape[3] // STEP
    return pl.pallas_call(
        decode_kernel,
        in_specs=[pl.BlockSpec(memory_space=pltpu.VMEM)] * 3,
        out_specs=pl.BlockSpec(memory_space=pl.ANY),
        out_shape=jax.ShapeDtypeStruct(weight.shape, weight.dtype),
        scratch_shapes=[
            pltpu.VMEM(weight.shape, weight.dtype),
            pltpu.SemaphoreType.DMA((steps,)),
        ],
        compiler_params=pltpu.CompilerParams(vmem_limit_bytes=24 * 1024 * 1024),
        name="decode",
    )(updates, basis_pieces, weight)


def local(activations, output_grads, basis, weight, first_moment, second_moment):
    core = lax.axis_index("c")
    piece = basis.shape[0] // 8
    which = jnp.full((1,), lax.axis_index("y") * 2 + core, jnp.int32)
    partial_product, mine = product(activations, basis, which, piece)
    partial_product, mine, first = lax.optimization_barrier((partial_product, mine, core == 0))
    rows, rank = partial_product.shape
    blocks = lax.all_to_all(
        partial_product.reshape(4, rows // 4, rank), "x", 0, 0, tiled=True
    )
    mine = lax.all_gather(mine, "zh", axis=0, tiled=True)
    blocks, mine = lax.optimization_barrier((blocks, mine))
    over_x = jnp.sum(blocks.astype(jnp.float32), axis=0).astype(jnp.bfloat16)
    basis_pieces = lax.all_gather(mine, ("y", "x", "c"), axis=0, tiled=True)
    basis_pieces = basis_pieces.reshape(4, 4, 2, 4, piece, rank)

    over_all = lax.all_gather(over_x, "zh", axis=0)
    block = jnp.sum(over_all.astype(jnp.float32), axis=0).astype(jnp.bfloat16)
    projected = gather(block, "x")
    local_term = (
        lax.dot_general(
            output_grads, projected, (((0,), (0,)), ((), ())), preferred_element_type=jnp.float32
        )
        / TOKENS
    )
    parts = local_term.reshape(-1, 2, 8, rank)
    keep = jnp.where(first, parts[:, 0], parts[:, 1])
    send = jnp.where(first, parts[:, 1], parts[:, 0]).astype(jnp.bfloat16)
    sent = lax.all_gather(send, "c", axis=0)
    received = jnp.where(first, sent[1], sent[0])
    chip_term = keep + received.astype(jnp.float32)
    low_grad = exchange_sum(chip_term.reshape(-1, rank), ("zl", "y"))
    new_first = first_decay * first_moment + (1.0 - first_decay) * low_grad
    new_second = second_decay * second_moment + (1.0 - second_decay) * low_grad * low_grad
    update = (new_first / first_fix / (jnp.sqrt(new_second / second_fix) + tiny_eps)).astype(
        jnp.bfloat16
    )
    updates = lax.all_gather(gather(update, ("zl", "y")), "c", axis=0)
    return (decode(updates, basis_pieces, weight), new_first, new_second)


def solution(mesh):
    named = Mesh(mesh.devices.reshape(SIZES), AXES)
    return jax.shard_map(
        local,
        mesh=named,
        in_specs=(
            P(DP, FSDP),
            P(DP, FSDP),
            P(FSDP, None),
            P(FSDP, None),
            P(FSDP + DP, None),
            P(FSDP + DP, None),
        ),
        out_specs=(P(FSDP, None), P(FSDP + DP, None), P(FSDP + DP, None)),
        check_vma=False,
    )
```

```python
import jax
import jax.numpy as jnp
from jax import lax
from jax.experimental import pallas as pl
from jax.experimental.pallas import tpu as pltpu
from jax.sharding import Mesh
from jax.sharding import PartitionSpec as P

first_decay = 0.9
second_decay = 0.999
first_fix = 1.0 - 0.9**10
second_fix = 1.0 - 0.999**10
step_rate = 0.01
tiny_eps = 1e-08

AXES = ("zl", "y", "c", "zh", "x")
SIZES = (4, 4, 2, 4, 4)
DP = ("zl", "y", "c")
FSDP = ("zh", "x")
TOKENS = 8192


def exchange_sum(value, axis):
    size = lax.axis_size(axis)
    rows, cols = value.shape
    parts = value.astype(jnp.bfloat16).reshape(size, rows // size, cols)
    parts = lax.all_to_all(parts, axis, 0, 0, tiled=True)
    return jnp.sum(parts.astype(jnp.float32), axis=0)


def gather(value, axis):
    size = lax.axis_size(axis)
    copies = jnp.broadcast_to(value[None], (size,) + value.shape)
    return lax.all_to_all(copies, axis, 0, 0, tiled=True).reshape(
        size * value.shape[0], value.shape[1]
    )


def product_kernel(start_ref, left_ref, right_ref, out_ref, piece_ref, left, right, out, sems):
    rows = piece_ref.shape[0]
    loads = [
        pltpu.make_async_copy(right_ref, right, sems.at[0]),
        pltpu.make_async_copy(left_ref, left, sems.at[1]),
    ]
    for load in loads:
        load.start()
    for load in loads:
        load.wait()
    where = pl.ds(pl.multiple_of(start_ref[0] * rows, rows), rows)
    piece = pltpu.make_async_copy(right.at[where], piece_ref, sems.at[2])
    piece.start()
    out[...] = jnp.dot(left[...], right[...], preferred_element_type=jnp.float32)
    store = pltpu.make_async_copy(out, out_ref, sems.at[3])
    store.start()
    piece.wait()
    store.wait()


def product(left, right, which, rows):
    shape = (left.shape[0], right.shape[1])
    anywhere = pl.BlockSpec(memory_space=pl.ANY)
    return pl.pallas_call(
        product_kernel,
        in_specs=[pl.BlockSpec(memory_space=pltpu.SMEM), anywhere, anywhere],
        out_specs=[anywhere, anywhere],
        out_shape=[
            jax.ShapeDtypeStruct(shape, jnp.float32),
            jax.ShapeDtypeStruct((rows, right.shape[1]), right.dtype),
        ],
        scratch_shapes=[
            pltpu.VMEM(left.shape, left.dtype),
            pltpu.VMEM(right.shape, right.dtype),
            pltpu.VMEM(shape, jnp.float32),
            pltpu.SemaphoreType.DMA((4,)),
        ],
        compiler_params=pltpu.CompilerParams(vmem_limit_bytes=60 * 1024 * 1024),
        name="product",
    )(which, left, right)


STEP = 2


def decode_kernel(update_ref, basis_ref, weight_ref, out_ref, new, sems):
    ys, xs, two, zhs, piece, rank = basis_ref.shape
    shard = two * ys * piece
    cols = STEP * shard

    def copy_out(i):
        where = pl.ds(i * cols, cols)
        return pltpu.make_async_copy(new.at[:, where], out_ref.at[:, where], sems.at[i])

    updates = update_ref[...].reshape(-1, rank)
    steps = xs * zhs // STEP
    for i in range(steps):
        shards = [
            basis_ref[:, f % xs, :, f // xs].reshape(shard, rank)
            for f in range(i * STEP, (i + 1) * STEP)
        ]
        decoded = lax.dot_general(
            updates,
            jnp.concatenate(shards, axis=0),
            (((1,), (1,)), ((), ())),
            preferred_element_type=jnp.float32,
        )
        decoded = decoded.reshape(2, -1, 8, cols)
        decoded = jnp.stack([decoded[0], decoded[1]], axis=1).reshape(-1, cols)
        old = weight_ref[:, i * cols : (i + 1) * cols].astype(jnp.float32)
        new[:, i * cols : (i + 1) * cols] = (old - step_rate * decoded).astype(new.dtype)
        copy_out(i).start()
    for i in range(steps):
        copy_out(i).wait()


def decode(updates, basis_pieces, weight):
    steps = basis_pieces.shape[1] * basis_pieces.shape[3] // STEP
    return pl.pallas_call(
        decode_kernel,
        in_specs=[pl.BlockSpec(memory_space=pltpu.VMEM)] * 3,
        out_specs=pl.BlockSpec(memory_space=pl.ANY),
        out_shape=jax.ShapeDtypeStruct(weight.shape, weight.dtype),
        scratch_shapes=[
            pltpu.VMEM(weight.shape, weight.dtype),
            pltpu.SemaphoreType.DMA((steps,)),
        ],
        compiler_params=pltpu.CompilerParams(vmem_limit_bytes=24 * 1024 * 1024),
        name="decode",
    )(updates, basis_pieces, weight)


def local(activations, output_grads, basis, weight, first_moment, second_moment):
    core = lax.axis_index("c")
    piece = basis.shape[0] // 8
    which = jnp.full((1,), lax.axis_index("y") * 2 + core, jnp.int32)
    partial_product, mine = product(activations, basis, which, piece)
    partial_product, mine, first = lax.optimization_barrier((partial_product, mine, core == 0))
    rows, rank = partial_product.shape
    blocks = lax.all_to_all(
        partial_product.reshape(4, rows // 4, rank), "x", 0, 0, tiled=True
    )
    mine = lax.all_gather(mine, "zh", axis=0, tiled=True)
    blocks, mine = lax.optimization_barrier((blocks, mine))
    over_x = jnp.sum(blocks, axis=0).astype(jnp.bfloat16)
    basis_pieces = lax.all_gather(mine, ("y", "x", "c"), axis=0, tiled=True)
    basis_pieces = basis_pieces.reshape(4, 4, 2, 4, piece, rank)

    over_all = lax.all_gather(over_x, "zh", axis=0)
    block = jnp.sum(over_all.astype(jnp.float32), axis=0).astype(jnp.bfloat16)
    projected = gather(block, "x")
    local_term = (
        lax.dot_general(
            output_grads, projected, (((0,), (0,)), ((), ())), preferred_element_type=jnp.float32
        )
        / TOKENS
    )
    parts = local_term.reshape(-1, 2, 8, rank)
    keep = jnp.where(first, parts[:, 0], parts[:, 1])
    send = jnp.where(first, parts[:, 1], parts[:, 0]).astype(jnp.bfloat16)
    sent = lax.all_gather(send, "c", axis=0)
    received = jnp.where(first, sent[1], sent[0])
    chip_term = keep + received.astype(jnp.float32)
    low_grad = exchange_sum(chip_term.reshape(-1, rank), ("zl", "y"))
    new_first = first_decay * first_moment + (1.0 - first_decay) * low_grad
    new_second = second_decay * second_moment + (1.0 - second_decay) * low_grad * low_grad
    update = (new_first / first_fix / (jnp.sqrt(new_second / second_fix) + tiny_eps)).astype(
        jnp.bfloat16
    )
    updates = lax.all_gather(gather(update, ("zl", "y")), "c", axis=0)
    return (decode(updates, basis_pieces, weight), new_first, new_second)


def solution(mesh):
    named = Mesh(mesh.devices.reshape(SIZES), AXES)
    return jax.shard_map(
        local,
        mesh=named,
        in_specs=(
            P(DP, FSDP),
            P(DP, FSDP),
            P(FSDP, None),
            P(FSDP, None),
            P(FSDP + DP, None),
            P(FSDP + DP, None),
        ),
        out_specs=(P(FSDP, None), P(FSDP + DP, None), P(FSDP + DP, None)),
        check_vma=False,
    )
```

```python
import jax
import jax.numpy as jnp
from jax import lax
from jax.experimental import pallas as pl
from jax.experimental.pallas import tpu as pltpu
from jax.sharding import Mesh
from jax.sharding import PartitionSpec as P

first_decay = 0.9
second_decay = 0.999
first_fix = 1.0 - 0.9**10
second_fix = 1.0 - 0.999**10
step_rate = 0.01
tiny_eps = 1e-08

AXES = ("zl", "y", "c", "zh", "x")
SIZES = (4, 4, 2, 4, 4)
DP = ("zl", "y", "c")
FSDP = ("zh", "x")
TOKENS = 8192


def exchange_sum(value, axis):
    size = lax.axis_size(axis)
    rows, cols = value.shape
    parts = value.astype(jnp.bfloat16).reshape(size, rows // size, cols)
    parts = lax.all_to_all(parts, axis, 0, 0, tiled=True)
    return jnp.sum(parts.astype(jnp.float32), axis=0)


def gather(value, axis):
    size = lax.axis_size(axis)
    copies = jnp.broadcast_to(value[None], (size,) + value.shape)
    return lax.all_to_all(copies, axis, 0, 0, tiled=True).reshape(
        size * value.shape[0], value.shape[1]
    )


def product_kernel(start_ref, left_ref, right_ref, out_ref, piece_ref, left, right, out, sems):
    rows = piece_ref.shape[0]
    loads = [
        pltpu.make_async_copy(right_ref, right, sems.at[0]),
        pltpu.make_async_copy(left_ref, left, sems.at[1]),
    ]
    for load in loads:
        load.start()
    for load in loads:
        load.wait()
    where = pl.ds(pl.multiple_of(start_ref[0] * rows, rows), rows)
    piece = pltpu.make_async_copy(right.at[where], piece_ref, sems.at[2])
    piece.start()
    out[...] = jnp.dot(left[...], right[...], preferred_element_type=jnp.float32)
    store = pltpu.make_async_copy(out, out_ref, sems.at[3])
    store.start()
    piece.wait()
    store.wait()


def product(left, right, which, rows):
    shape = (left.shape[0], right.shape[1])
    anywhere = pl.BlockSpec(memory_space=pl.ANY)
    return pl.pallas_call(
        product_kernel,
        in_specs=[pl.BlockSpec(memory_space=pltpu.SMEM), anywhere, anywhere],
        out_specs=[anywhere, anywhere],
        out_shape=[
            jax.ShapeDtypeStruct(shape, jnp.float32),
            jax.ShapeDtypeStruct((rows, right.shape[1]), right.dtype),
        ],
        scratch_shapes=[
            pltpu.VMEM(left.shape, left.dtype),
            pltpu.VMEM(right.shape, right.dtype),
            pltpu.VMEM(shape, jnp.float32),
            pltpu.SemaphoreType.DMA((4,)),
        ],
        compiler_params=pltpu.CompilerParams(vmem_limit_bytes=60 * 1024 * 1024),
        name="product",
    )(which, left, right)


STEP = 2


def decode_kernel(update_ref, basis_ref, weight_ref, out_ref, held, new, in_sems, out_sems):
    ys, xs, two, zhs, piece, rank = basis_ref.shape
    shard = two * ys * piece
    parts = [(x, z) for x in range(xs) for z in range(0, zhs, STEP)]

    def copy_in(i):
        x, z = parts[i]
        return pltpu.make_async_copy(
            basis_ref.at[:, x, :, pl.ds(z, STEP)], held.at[i], in_sems.at[i]
        )

    def copy_out(i, k):
        x, z = parts[i]
        where = pl.ds(((z + k) * xs + x) * shard, shard)
        return pltpu.make_async_copy(
            new.at[:, where], out_ref.at[:, where], out_sems.at[i * STEP + k]
        )

    for i in range(len(parts)):
        copy_in(i).start()
    updates = update_ref[...].reshape(-1, rank)
    for i, (x, z) in enumerate(parts):
        copy_in(i).wait()
        shards = [held[i, :, :, k].reshape(shard, rank) for k in range(STEP)]
        decoded = lax.dot_general(
            updates,
            jnp.concatenate(shards, axis=0),
            (((1,), (1,)), ((), ())),
            preferred_element_type=jnp.float32,
        )
        decoded = decoded.reshape(2, -1, 8, STEP * shard)
        decoded = jnp.stack([decoded[0], decoded[1]], axis=1).reshape(-1, STEP * shard)
        for k in range(STEP):
            start = ((z + k) * xs + x) * shard
            old = weight_ref[:, start : start + shard].astype(jnp.float32)
            new[:, start : start + shard] = (
                old - step_rate * decoded[:, k * shard : (k + 1) * shard]
            ).astype(new.dtype)
            copy_out(i, k).start()
    for i in range(len(parts)):
        for k in range(STEP):
            copy_out(i, k).wait()


def decode(updates, basis_pieces, weight):
    ys, xs, two, zhs, piece, rank = basis_pieces.shape
    steps = xs * zhs // STEP
    vmem = pl.BlockSpec(memory_space=pltpu.VMEM)
    anywhere = pl.BlockSpec(memory_space=pl.ANY)
    return pl.pallas_call(
        decode_kernel,
        in_specs=[vmem, anywhere, vmem],
        out_specs=anywhere,
        out_shape=jax.ShapeDtypeStruct(weight.shape, weight.dtype),
        scratch_shapes=[
            pltpu.VMEM((steps, ys, two, STEP, piece, rank), basis_pieces.dtype),
            pltpu.VMEM(weight.shape, weight.dtype),
            pltpu.SemaphoreType.DMA((steps,)),
            pltpu.SemaphoreType.DMA((steps * STEP,)),
        ],
        compiler_params=pltpu.CompilerParams(vmem_limit_bytes=46 * 1024 * 1024),
        name="decode",
    )(updates, basis_pieces, weight)


def local(activations, output_grads, basis, weight, first_moment, second_moment):
    core = lax.axis_index("c")
    piece = basis.shape[0] // 8
    which = jnp.full((1,), lax.axis_index("y") * 2 + core, jnp.int32)
    partial_product, mine = product(activations, basis, which, piece)
    partial_product, mine, first = lax.optimization_barrier((partial_product, mine, core == 0))
    rows, rank = partial_product.shape
    blocks = lax.all_to_all(
        partial_product.reshape(4, rows // 4, rank), "x", 0, 0, tiled=True
    )
    mine = lax.all_gather(mine, "zh", axis=0, tiled=True)
    blocks, mine = lax.optimization_barrier((blocks, mine))
    over_x = jnp.sum(blocks, axis=0).astype(jnp.bfloat16)
    basis_pieces = lax.all_gather(mine, ("y", "x", "c"), axis=0, tiled=True)
    basis_pieces = basis_pieces.reshape(4, 4, 2, 4, piece, rank)

    over_all = lax.all_gather(over_x, "zh", axis=0)
    block = jnp.sum(over_all.astype(jnp.float32), axis=0).astype(jnp.bfloat16)
    projected = gather(block, "x")
    local_term = (
        lax.dot_general(
            output_grads, projected, (((0,), (0,)), ((), ())), preferred_element_type=jnp.float32
        )
        / TOKENS
    )
    parts = local_term.reshape(-1, 2, 8, rank)
    keep = jnp.where(first, parts[:, 0], parts[:, 1])
    send = jnp.where(first, parts[:, 1], parts[:, 0]).astype(jnp.bfloat16)
    sent = lax.all_gather(send, "c", axis=0)
    received = jnp.where(first, sent[1], sent[0])
    chip_term = keep + received.astype(jnp.float32)
    low_grad = exchange_sum(chip_term.reshape(-1, rank), ("zl", "y"))
    new_first = first_decay * first_moment + (1.0 - first_decay) * low_grad
    new_second = second_decay * second_moment + (1.0 - second_decay) * low_grad * low_grad
    update = (new_first / first_fix / (jnp.sqrt(new_second / second_fix) + tiny_eps)).astype(
        jnp.bfloat16
    )
    updates = lax.all_gather(gather(update, ("zl", "y")), "c", axis=0)
    return (decode(updates, basis_pieces, weight), new_first, new_second)


def solution(mesh):
    named = Mesh(mesh.devices.reshape(SIZES), AXES)
    return jax.shard_map(
        local,
        mesh=named,
        in_specs=(
            P(DP, FSDP),
            P(DP, FSDP),
            P(FSDP, None),
            P(FSDP, None),
            P(FSDP + DP, None),
            P(FSDP + DP, None),
        ),
        out_specs=(P(FSDP, None), P(FSDP + DP, None), P(FSDP + DP, None)),
        check_vma=False,
    )
```

```python
import jax
import jax.numpy as jnp
from jax import lax
from jax.experimental import pallas as pl
from jax.experimental.pallas import tpu as pltpu
from jax.sharding import Mesh
from jax.sharding import PartitionSpec as P

first_decay = 0.9
second_decay = 0.999
first_fix = 1.0 - 0.9**10
second_fix = 1.0 - 0.999**10
step_rate = 0.01
tiny_eps = 1e-08

AXES = ("zl", "y", "c", "zh", "x")
SIZES = (4, 4, 2, 4, 4)
DP = ("zl", "y", "c")
FSDP = ("zh", "x")
TOKENS = 8192


def exchange_sum(value, axis):
    size = lax.axis_size(axis)
    rows, cols = value.shape
    parts = value.astype(jnp.bfloat16).reshape(size, rows // size, cols)
    parts = lax.all_to_all(parts, axis, 0, 0, tiled=True)
    return jnp.sum(parts.astype(jnp.float32), axis=0)


def gather(value, axis):
    size = lax.axis_size(axis)
    copies = jnp.broadcast_to(value[None], (size,) + value.shape)
    return lax.all_to_all(copies, axis, 0, 0, tiled=True).reshape(
        size * value.shape[0], value.shape[1]
    )


BLOCKS = 4


def product_kernel(start_ref, left_ref, right_ref, out_ref, piece_ref, left, right, out, sems):
    rows = piece_ref.shape[0]
    loads = [
        pltpu.make_async_copy(right_ref, right, sems.at[0]),
        pltpu.make_async_copy(left_ref, left, sems.at[1]),
    ]
    for load in loads:
        load.start()
    for load in loads:
        load.wait()
    where = pl.ds(pl.multiple_of(start_ref[0] * rows, rows), rows)
    piece = pltpu.make_async_copy(right.at[where], piece_ref, sems.at[2])
    piece.start()
    stores = []
    step = out.shape[0] // BLOCKS
    for i in range(BLOCKS):
        block = pl.ds(i * step, step)
        out[block] = jnp.dot(left[block], right[...], preferred_element_type=jnp.float32)
        store = pltpu.make_async_copy(out.at[block], out_ref.at[block], sems.at[3 + i])
        store.start()
        stores.append(store)
    piece.wait()
    for store in stores:
        store.wait()


def product(left, right, which, rows):
    shape = (left.shape[0], right.shape[1])
    anywhere = pl.BlockSpec(memory_space=pl.ANY)
    return pl.pallas_call(
        product_kernel,
        in_specs=[pl.BlockSpec(memory_space=pltpu.SMEM), anywhere, anywhere],
        out_specs=[anywhere, anywhere],
        out_shape=[
            jax.ShapeDtypeStruct(shape, jnp.float32),
            jax.ShapeDtypeStruct((rows, right.shape[1]), right.dtype),
        ],
        scratch_shapes=[
            pltpu.VMEM(left.shape, left.dtype),
            pltpu.VMEM(right.shape, right.dtype),
            pltpu.VMEM(shape, jnp.float32),
            pltpu.SemaphoreType.DMA((3 + BLOCKS,)),
        ],
        compiler_params=pltpu.CompilerParams(vmem_limit_bytes=60 * 1024 * 1024),
        name="product",
    )(which, left, right)


STEP = 2


def decode_kernel(update_ref, basis_ref, weight_ref, out_ref, held, new, in_sems, out_sems):
    ys, xs, two, zhs, piece, rank = basis_ref.shape
    shard = two * ys * piece
    parts = [(x, z) for x in range(xs) for z in range(0, zhs, STEP)]

    def copy_in(i):
        x, z = parts[i]
        return pltpu.make_async_copy(
            basis_ref.at[:, x, :, pl.ds(z, STEP)], held.at[i], in_sems.at[i]
        )

    def copy_out(i, k):
        x, z = parts[i]
        where = pl.ds(((z + k) * xs + x) * shard, shard)
        return pltpu.make_async_copy(
            new.at[:, where], out_ref.at[:, where], out_sems.at[i * STEP + k]
        )

    for i in range(len(parts)):
        copy_in(i).start()
    updates = update_ref[...].reshape(-1, rank)
    for i, (x, z) in enumerate(parts):
        copy_in(i).wait()
        shards = [held[i, :, :, k].reshape(shard, rank) for k in range(STEP)]
        decoded = lax.dot_general(
            updates,
            jnp.concatenate(shards, axis=0),
            (((1,), (1,)), ((), ())),
            preferred_element_type=jnp.float32,
        )
        decoded = decoded.reshape(2, -1, 8, STEP * shard)
        decoded = jnp.stack([decoded[0], decoded[1]], axis=1).reshape(-1, STEP * shard)
        for k in range(STEP):
            start = ((z + k) * xs + x) * shard
            old = weight_ref[:, start : start + shard].astype(jnp.float32)
            new[:, start : start + shard] = (
                old - step_rate * decoded[:, k * shard : (k + 1) * shard]
            ).astype(new.dtype)
            copy_out(i, k).start()
    for i in range(len(parts)):
        for k in range(STEP):
            copy_out(i, k).wait()


def decode(updates, basis_pieces, weight):
    ys, xs, two, zhs, piece, rank = basis_pieces.shape
    steps = xs * zhs // STEP
    vmem = pl.BlockSpec(memory_space=pltpu.VMEM)
    anywhere = pl.BlockSpec(memory_space=pl.ANY)
    return pl.pallas_call(
        decode_kernel,
        in_specs=[vmem, anywhere, vmem],
        out_specs=anywhere,
        out_shape=jax.ShapeDtypeStruct(weight.shape, weight.dtype),
        scratch_shapes=[
            pltpu.VMEM((steps, ys, two, STEP, piece, rank), basis_pieces.dtype),
            pltpu.VMEM(weight.shape, weight.dtype),
            pltpu.SemaphoreType.DMA((steps,)),
            pltpu.SemaphoreType.DMA((steps * STEP,)),
        ],
        compiler_params=pltpu.CompilerParams(vmem_limit_bytes=46 * 1024 * 1024),
        name="decode",
    )(updates, basis_pieces, weight)


def local(activations, output_grads, basis, weight, first_moment, second_moment):
    core = lax.axis_index("c")
    piece = basis.shape[0] // 8
    which = jnp.full((1,), lax.axis_index("y") * 2 + core, jnp.int32)
    partial_product, mine = product(activations, basis, which, piece)
    partial_product, mine, first = lax.optimization_barrier((partial_product, mine, core == 0))
    rows, rank = partial_product.shape
    blocks = lax.all_to_all(
        partial_product.reshape(4, rows // 4, rank), "x", 0, 0, tiled=True
    )
    mine = lax.all_gather(mine, "zh", axis=0, tiled=True)
    blocks, mine = lax.optimization_barrier((blocks, mine))
    over_x = jnp.sum(blocks, axis=0).astype(jnp.bfloat16)
    basis_pieces = lax.all_gather(mine, ("y", "x", "c"), axis=0, tiled=True)
    basis_pieces = basis_pieces.reshape(4, 4, 2, 4, piece, rank)

    over_all = lax.all_gather(over_x, "zh", axis=0)
    block = jnp.sum(over_all.astype(jnp.float32), axis=0).astype(jnp.bfloat16)
    projected = gather(block, "x")
    local_term = (
        lax.dot_general(
            output_grads, projected, (((0,), (0,)), ((), ())), preferred_element_type=jnp.float32
        )
        / TOKENS
    )
    parts = local_term.reshape(-1, 2, 8, rank)
    keep = jnp.where(first, parts[:, 0], parts[:, 1])
    send = jnp.where(first, parts[:, 1], parts[:, 0]).astype(jnp.bfloat16)
    sent = lax.all_gather(send, "c", axis=0)
    received = jnp.where(first, sent[1], sent[0])
    chip_term = keep + received.astype(jnp.float32)
    low_grad = exchange_sum(chip_term.reshape(-1, rank), ("zl", "y"))
    new_first = first_decay * first_moment + (1.0 - first_decay) * low_grad
    new_second = second_decay * second_moment + (1.0 - second_decay) * low_grad * low_grad
    update = (new_first / first_fix / (jnp.sqrt(new_second / second_fix) + tiny_eps)).astype(
        jnp.bfloat16
    )
    updates = lax.all_gather(gather(update, ("zl", "y")), "c", axis=0)
    return (decode(updates, basis_pieces, weight), new_first, new_second)


def solution(mesh):
    named = Mesh(mesh.devices.reshape(SIZES), AXES)
    return jax.shard_map(
        local,
        mesh=named,
        in_specs=(
            P(DP, FSDP),
            P(DP, FSDP),
            P(FSDP, None),
            P(FSDP, None),
            P(FSDP + DP, None),
            P(FSDP + DP, None),
        ),
        out_specs=(P(FSDP, None), P(FSDP + DP, None), P(FSDP + DP, None)),
        check_vma=False,
    )
```
